1024 devices in a mesh: pop: 16 (over y, z_hi), fsdp: 64 (over x, z_lo, core).
Axes of the slice: x: 4, y: 8, z: 16 (z_hi: 2, z_lo: 8; z = z_hi * 8 + z_lo), core: 2. Of those that a mesh axis runs over, the one named last changes fastest.
Arguments:
- weight: float32 [14336, 8192], P('fsdp', 'pop'), may hold values from -6 to 6
- first_moment: float32 [14336, 8192], P('fsdp', 'pop'), may hold values from -4 to 4
- second_moment: float32 [14336, 8192], P('fsdp', 'pop'), may hold values from 0.0001 to 0.01
- row_factors: bfloat16 [1024, 4, 14336], P('pop', None, 'fsdp'), may hold values from -6 to 6
- column_factors: bfloat16 [1024, 4, 8192], P(None, None, ('pop', 'fsdp')), may hold values from -6 to 6
- scores: int32 [1024], P('pop'), may hold values from 0 to 799, as said below
Outputs:
- new_weight: float32 [14336, 8192], P('fsdp', 'pop')
- new_first: float32 [14336, 8192], P('fsdp', 'pop')
- new_second: float32 [14336, 8192], P('fsdp', 'pop')
The draws below stay inside these ranges and needn't reach their ends.
Inputs may be any that keep to these rules, and one draw needn't show every extreme that they name: Integer fitness scores; the lowest and the highest possible score both occur.
All inputs are finite; a program needn't handle non-finite values.
Results may differ from the reference program's by a relative error of at most 0.0017.
Values may be sent and summed in bfloat16 or wider, within the bound.
A program may use at most 32 MiB of HBM per device.

```python
import math
import jax
import jax.numpy as jnp
from jax import lax

D = 8192
FF = 14336
RANK = 4
ADAM_STEP = 10
MEMBERS = 1024


def draw_scores(key, part):
    key = jax.random.fold_in(key, 7)
    member_index = jnp.arange(MEMBERS, dtype=jnp.int32)
    ceiling = 200 + 600 * member_index // MEMBERS
    drawn = jax.random.randint(key, (MEMBERS,), 0, ceiling, dtype=jnp.int32)
    drawn = jnp.where(member_index == 0, jnp.int32(0), drawn)
    drawn = jnp.where(member_index == MEMBERS - 1, jnp.int32(799), drawn)
    return drawn


def levels(own_key, shape, pieces, least, high):
    factor_of = 1.0
    for axis_at, blocks in pieces:
        steps = jax.random.uniform(jax.random.fold_in(jax.random.fold_in(own_key, 6), axis_at), (blocks,), jnp.float32, least / len(pieces), high / len(pieces))
        factor_of = factor_of * jnp.repeat(jnp.exp(steps), shape[axis_at] // blocks).reshape((-1,) + (1,) * (len(shape) - 1 - axis_at))
    return factor_of


def centred(stream_key, extent, width, limit, split=(), held_as=jnp.bfloat16):
    factor_of = levels(stream_key, extent, split, -0.22, 0.18) if split else 1.0
    values = jax.random.normal(stream_key, extent, jnp.float32) * width * factor_of
    return jnp.minimum(jnp.maximum(values, -limit), limit).astype(held_as)


def setup_inputs(seed: int = 0) -> dict:
    key_list = jax.random.split(jax.random.key(seed), 7)
    return {
        "weight": centred(key_list[0], (FF, D), 1.0, 6.0, ((0, 64), (1, 16)), jnp.float32),
        "first_moment": centred(key_list[1], (FF, D), 0.3, 4.0, ((0, 64), (1, 16)), jnp.float32),
        "second_moment": jnp.clip(jnp.exp(math.log(0.01) - 4.6051702 * jax.random.uniform(key_list[2], (FF, D), jnp.float32) ** levels(key_list[2], (FF, D), ((0, 64), (1, 16)), -0.2, 0.2)), 0.0001, 0.01),
        "row_factors": centred(key_list[3], (MEMBERS, RANK, FF), 1.0, 6.0, ((0, 16), (2, 64))),
        "column_factors": centred(key_list[4], (MEMBERS, RANK, D), 1.0, 6.0, ((2, 1024),)),
        "scores": draw_scores(jax.random.fold_in(key_list[6], 71), 0),
    }


beta_one = 0.9
beta_two = 0.999
learn_rate = 0.05
adam_eps = 1e-08
score_eps = 1e-05

def reference(weight, first_moment, second_moment, row_factors, column_factors, scores):
    values = scores.astype(jnp.float32)
    average = jnp.sum(values) / MEMBERS
    variance = jnp.sum(values * values) / MEMBERS - average * average
    fitness = (values - average) * lax.rsqrt(variance + score_eps)
    weighted = (fitness[:, None, None] * row_factors.astype(jnp.float32)).astype(jnp.bfloat16)
    left_rows = weighted.astype(jnp.float32).reshape(MEMBERS * RANK, FF)
    right_rows = column_factors.astype(jnp.float32).reshape(MEMBERS * RANK, D)
    update = lax.dot_general(left_rows, right_rows, (((0,), (0,)), ((), ())), precision=lax.Precision.HIGHEST, preferred_element_type=jnp.float32)
    update = update / math.sqrt(MEMBERS * RANK)
    new_first = beta_one * first_moment + (1.0 - beta_one) * update
    new_second = beta_two * second_moment + (1.0 - beta_two) * update * update
    corrected_first = new_first / (1.0 - beta_one ** ADAM_STEP)
    corrected_second = new_second / (1.0 - beta_two ** ADAM_STEP)
    new_weight = weight + learn_rate * corrected_first / (jnp.sqrt(corrected_second) + adam_eps)
    return (new_weight, new_first, new_second)
```

```python
import functools
import math

import jax
import jax.numpy as jnp
from jax import lax
from jax.experimental import pallas as pl
from jax.experimental.pallas import tpu as pltpu
from jax.sharding import PartitionSpec as P

ADAM_STEP = 10
MESH = pl.DeviceIdType.MESH

beta_one = 0.9
beta_two = 0.999
learn_rate = 0.05
adam_eps = 1e-08
score_eps = 1e-05

NX, NY, NZ, RUN = 4, 8, 16, 8
POP = 16
ROWS = 224
COLS = 512
KEEP = 2048
SLOT = 2 * ROWS + 16
T_Y, T_Z4, T_C, T_C4, T_X, T_SIB = 3.3, 5.5, 3.0, 4.5, 3.0, 1.5


def device_at(x, y, z, c):
    x, y, z = (x + NX) % NX, (y + NY) % NY, (z + NZ) % NZ
    return (y * 2 + z // RUN, (x * RUN + z % RUN) * 2 + c)


def swap_lanes(even, odd):
    low = lax.broadcasted_iota(jnp.int32, (even.shape[0], 128), 1) < 64
    parts = []
    for t in range(8):
        a = even[:, t * 128 : (t + 1) * 128]
        b = odd[:, t * 128 : (t + 1) * 128]
        parts.append(jnp.where(low, a, pltpu.roll(b, 64, 1)))
        parts.append(jnp.where(low, pltpu.roll(a, 64, 1), b))
    return jnp.concatenate(parts, axis=1)


def kernel(
    row_ref, col_ref, score_ref, out_ref,
    rowbuf, transit, colbuf, row_out, col_out, col_in, wbuf, part_out, part_in,
    sem_sib_s, sem_sib_r, sem_z4_s, sem_z4_r, sem_y_s, sem_y_r,
    sem_c_s, sem_c_r, sem_x_s, sem_x_r, sem_f_s, sem_f_r,
):
    p = lax.axis_index("pop")
    f = lax.axis_index("fsdp")
    y, zh = p // 2, p % 2
    c, zl, x = f % 2, (f // 2) % RUN, f // (2 * RUN)
    z = zh * RUN + zl
    turn = 1 - 2 * c

    partners = [
        device_at(x, y, z, 1 - c),
        device_at(x, y + 1, z, c), device_at(x, y + NY - 1, z, c),
        device_at(x + 1, y, z, c), device_at(x + NX - 1, y, z, c),
        device_at(x, y, z + 1, c), device_at(x, y, z + NZ - 1, c),
        device_at(x, y, z + 4, c), device_at(x, y, z + NZ - 4, c),
    ]
    sibling = partners[0]
    barrier = pltpu.get_barrier_semaphore()
    for dev in partners:
        pl.semaphore_signal(barrier, inc=1, device_id=dev, device_id_type=MESH)

    rows = jnp.swapaxes(row_ref[...], 0, 1)
    halves = [rows[2 * q : 2 * q + 2].reshape(128, ROWS).T for q in range(2)]
    mine = jnp.where(c == 0, halves[0], halves[1])
    theirs = jnp.where(c == 0, halves[1], halves[0])
    own_rows = pl.multiple_of(c * (ROWS + 16), 16)
    rowbuf[p, pl.ds(own_rows, ROWS), :] = mine
    row_out[...] = theirs
    score = score_ref[...]
    score = jnp.concatenate([score, score], axis=1)
    line = lax.broadcasted_iota(jnp.int32, (16, 128), 0)
    coded = jnp.where(line == 0, score // 16, jnp.where(line == 1, score % 16, 0))
    rowbuf[p, ROWS : ROWS + 16, :] = coded.astype(jnp.float32).astype(jnp.bfloat16)
    blocks = [col_ref[k].astype(jnp.float32) for k in range(4)]
    wide = [swap_lanes(blocks[2 * q], blocks[2 * q + 1]) for q in range(2)]
    my_cols = jnp.where(c == 0, wide[0], wide[1])
    col_out[...] = jnp.where(c == 0, wide[1], wide[0]).astype(jnp.bfloat16)

    pl.semaphore_wait(barrier, len(partners))

    sends = []

    def remote(src, dst, s_sem, r_sem, dev):
        return pltpu.make_async_remote_copy(
            src_ref=src, dst_ref=dst, send_sem=s_sem, recv_sem=r_sem, device_id=dev, device_id_type=MESH
        )

    def go(copy, when=None):
        if when is None:
            copy.start()
        else:
            pl.when(when)(copy.start)
        sends.append((when, copy))

    first_len = ROWS + 16

    def piece(buf, slot, n):
        if n == 0:
            start, length = c * ROWS, first_len
        else:
            start, length = (1 - c) * first_len, ROWS
        start = pl.multiple_of(start, 16)
        return buf.at[pl.ds(start, length)] if slot is None else buf.at[slot, pl.ds(start, length)]

    def y_copy(stream, way, hop, n):
        d = turn if way == 0 else -turn
        src_y = (y - d * (hop - 1) + 2 * NY) % NY
        slot = src_y * 2 + (zh if stream == 0 else 1 - zh)
        ref = piece(rowbuf, slot, n)
        i = stream * 2 + way
        return remote(ref, ref, sem_y_s.at[i, hop - 1, n], sem_y_r.at[i, hop - 1, n], device_at(x, y + d, z, c))

    def y_wait(stream, way, hop, n):
        y_copy(stream, way, hop, n).wait_recv()

    far = device_at(x, y, z + 4 * turn + NZ, c)
    behind = (z - 4 * turn + NZ) % NZ

    def z4_copy(stage, n):
        if stage == 0:
            src, dst = piece(rowbuf, p, n), piece(transit, None, n)
        else:
            src, dst = piece(transit, None, n), piece(rowbuf, y * 2 + behind // RUN, n)
        return remote(src, dst, sem_z4_s.at[stage, n], sem_z4_r.at[stage, n], far)

    def col_block(x_at, zl_at, half=None):
        at = pl.ds(pl.multiple_of((x_at * RUN + zl_at) * 16, 16), 16)
        if half is None:
            return colbuf.at[at]
        return colbuf.at[at, pl.ds(half * (KEEP // 2), KEEP // 2)]

    def c_copy(way, d):
        step = 1 - 2 * way
        origin = zl - step * (0 if d == 4 else d - 1)
        ref = col_block(x, origin)
        jump = 4 if d == 4 else 1
        return remote(ref, ref, sem_c_s.at[way, d - 1], sem_c_r.at[way, d - 1], device_at(x, y, z + step * jump + NZ, c))

    def inside(v):
        return jnp.logical_and(v >= 0, v < RUN)

    def c_send(way, d):
        step = 1 - 2 * way
        origin = zl - step * (0 if d == 4 else d - 1)
        target = zl + step * (4 if d == 4 else 1)
        go(c_copy(way, d), jnp.logical_and(inside(origin), inside(target)))

    def c_origin(way, d):
        return zl - (1 - 2 * way) * d

    def x_send(zl_at, when):
        for way in range(2):
            step = 1 - 2 * way
            ref = col_block(x, zl_at)
            at = jnp.clip(zl_at, 0, RUN - 1)
            go(remote(ref, ref, sem_x_s.at[way, at], sem_x_r.at[way, at], device_at(x + step + NX, y, z, c)), when)

    def x_pass(zl_at, when):
        for way in range(2):
            step = 1 - 2 * way
            at = jnp.clip(zl_at, 0, RUN - 1)
            x_at = (x - step + NX) % NX
            ref = col_block(x_at, zl_at)
            got = remote(ref, ref, sem_x_s.at[way, at], sem_x_r.at[way, at], device_at(x + step + NX, y, z, c))
            half = col_block(x_at, zl_at, way)
            on = remote(half, half, sem_f_s.at[way, at], sem_f_r.at[way, at], device_at(x + step + NX, y, z, c))
            if when is None:
                got.wait_recv()
            else:
                pl.when(when)(got.wait_recv)
            go(on, when)

    events = []

    def at_time(t, fn):
        events.append((t, len(events), fn))

    sib_rows = remote(row_out, rowbuf.at[p, pl.ds(own_rows, ROWS)], sem_sib_s.at[0], sem_sib_r.at[0], sibling)
    sib_cols = remote(col_out, col_in, sem_sib_s.at[1], sem_sib_r.at[1], sibling)

    def start():
        go(sib_cols)
        go(sib_rows)
        go(z4_copy(0, 0))
        go(y_copy(0, 0, 1, 0))
        go(y_copy(0, 1, 1, 0))

    def columns():
        sib_cols.wait_recv()
        other = col_in[...].astype(jnp.float32)
        both = jnp.concatenate([jnp.where(c == 0, my_cols, other), jnp.where(c == 0, other, my_cols)], axis=0)
        col_block(x, zl)[...] = both.astype(jnp.bfloat16)
        for d in (1, 4):
            for way in range(2):
                c_send(way, d)
        x_send(zl, None)

    def rows_second():
        sib_rows.wait_recv()
        go(z4_copy(0, 1))
        go(y_copy(0, 0, 1, 1))
        go(y_copy(0, 1, 1, 1))

    at_time(0.0, start)
    at_time(T_SIB, columns)
    at_time(T_SIB + 0.3, rows_second)

    def y_event(stream, way, hop, n):
        y_wait(stream, way, hop, n)
        if hop < (4 if way == 0 else 3):
            go(y_copy(stream, way, hop + 1, n))

    def z4_event(stage, n):
        z4_copy(stage, n).wait_recv()
        if stage == 0:
            go(z4_copy(1, n))
        else:
            go(y_copy(1, 0, 1, n))
            go(y_copy(1, 1, 1, n))

    for n in range(2):
        t0 = 0.0 if n == 0 else T_SIB + 0.3
        for stage in range(2):
            at_time(t0 + T_Z4 * (stage + 1), functools.partial(z4_event, stage, n))
        for stream in range(2):
            base = t0 + (0.0 if stream == 0 else 2 * T_Z4)
            for hop in range(1, 5):
                for way in range(2):
                    if hop <= (4 if way == 0 else 3):
                        at_time(base + T_Y * hop, functools.partial(y_event, stream, way, hop, n))

    def c_event(way, d):
        origin = c_origin(way, d)
        valid = inside(origin)
        step = 1 - 2 * way
        ref = col_block(x, origin)
        got = remote(
            ref, ref, sem_c_s.at[way, d - 1], sem_c_r.at[way, d - 1], device_at(x, y, z + step + NZ, c)
        )
        pl.when(valid)(got.wait_recv)
        if d not in (3, 7):
            c_send(way, d + 1)
        x_send(origin, valid)

    def x_event(way, d):
        origin = c_origin(way, d)
        x_pass(origin, inside(origin))

    at_time(T_SIB + T_X, lambda: x_pass(zl, None))
    for d in range(1, 8):
        for way in range(2):
            t = T_SIB + (T_C * d if d < 4 else T_C4 + T_C * (d - 4))
            at_time(t, functools.partial(c_event, way, d))
            at_time(t + T_X, functools.partial(x_event, way, d))

    for _, _, fn in sorted(events, key=lambda e: e[:2]):
        fn()

    for way in range(2):
        step = 1 - 2 * way
        for zl_at in range(RUN):
            half = col_block((x + 2) % NX, zl_at, way)
            remote(
                half, half, sem_f_s.at[way, zl_at], sem_f_r.at[way, zl_at], device_at(x + step + NX, y, z, c)
            ).wait_recv()

    tags = [rowbuf[i, ROWS : ROWS + 16, :].astype(jnp.float32) for i in range(POP)]
    values = [t[0:1] * 16.0 + t[1:2] for t in tags]
    values = jnp.concatenate(values, axis=0)
    members = POP * 64
    average = jnp.sum(values) * 0.5 / members
    variance = jnp.sum(values * values) * 0.5 / members - average * average
    fitness = (values - average) * lax.rsqrt(variance + score_eps)

    for i in range(POP):
        for h in range(2):
            block = rowbuf[i, h * first_len : h * first_len + ROWS, :].astype(jnp.float32)
            wbuf[h, :, i * 128 : (i + 1) * 128] = (block * fitness[i : i + 1]).astype(jnp.bfloat16)

    def product(h):
        return lax.dot_general(
            wbuf[h], colbuf[...], (((1,), (1,)), ((), ())), preferred_element_type=jnp.float32
        )

    part_out[...] = product(1 - c)
    swap = remote(part_out, part_in, sem_sib_s.at[2], sem_sib_r.at[2], sibling)
    swap.start()
    own = product(c)
    for when, copy in sends:
        if when is None:
            copy.wait_send()
        else:
            pl.when(when)(copy.wait_send)
    swap.wait()
    out_ref[...] = (own + part_in[...]) * (1.0 / 64.0)


def local(weight, first_moment, second_moment, row_factors, column_factors, scores):
    columns = jnp.transpose(column_factors, (1, 2, 0))
    dma = pltpu.SemaphoreType.DMA
    update = pl.pallas_call(
        kernel,
        name="gather_update",
        out_shape=jax.ShapeDtypeStruct((ROWS, COLS), jnp.float32),
        in_specs=[pl.BlockSpec(memory_space=pltpu.VMEM)] * 3,
        out_specs=pl.BlockSpec(memory_space=pltpu.VMEM),
        scratch_shapes=[
            pltpu.VMEM((POP, SLOT, 128), jnp.bfloat16),
            pltpu.VMEM((SLOT, 128), jnp.bfloat16),
            pltpu.VMEM((COLS, KEEP), jnp.bfloat16),
            pltpu.VMEM((ROWS, 128), jnp.bfloat16),
            pltpu.VMEM((8, KEEP), jnp.bfloat16),
            pltpu.VMEM((8, KEEP), jnp.bfloat16),
            pltpu.VMEM((2, ROWS, KEEP), jnp.bfloat16),
            pltpu.VMEM((ROWS, COLS), jnp.float32),
            pltpu.VMEM((ROWS, COLS), jnp.float32),
            dma((3,)), dma((3,)),
            dma((2, 2)), dma((2, 2)),
            dma((4, 4, 2)), dma((4, 4, 2)),
            dma((2, 7)), dma((2, 7)),
            dma((2, RUN)), dma((2, RUN)),
            dma((2, RUN)), dma((2, RUN)),
        ],
        compiler_params=pltpu.CompilerParams(
            collective_id=0, has_side_effects=True, vmem_limit_bytes=40 * 2**20
        ),
        cost_estimate=pl.CostEstimate(flops=2 * ROWS * COLS * 4096, bytes_accessed=2**20, transcendentals=0),
    )(row_factors, columns, scores.reshape(1, 64))
    new_first = beta_one * first_moment + (1.0 - beta_one) * update
    new_second = beta_two * second_moment + (1.0 - beta_two) * update * update
    corrected_first = new_first / (1.0 - beta_one**ADAM_STEP)
    corrected_second = new_second / (1.0 - beta_two**ADAM_STEP)
    new_weight = weight + learn_rate * corrected_first / (jnp.sqrt(corrected_second) + adam_eps)
    return (new_weight, new_first, new_second)


def solution(mesh):
    in_specs = (
        P("fsdp", "pop"),
        P("fsdp", "pop"),
        P("fsdp", "pop"),
        P("pop", None, "fsdp"),
        P(None, None, ("pop", "fsdp")),
        P("pop"),
    )
    out_specs = (P("fsdp", "pop"), P("fsdp", "pop"), P("fsdp", "pop"))
    return jax.shard_map(local, mesh=mesh, in_specs=in_specs, out_specs=out_specs, check_vma=False)
```

```python
import functools
import math

import jax
import jax.numpy as jnp
from jax import lax
from jax.experimental import pallas as pl
from jax.experimental.pallas import tpu as pltpu
from jax.sharding import PartitionSpec as P

ADAM_STEP = 10
MESH = pl.DeviceIdType.MESH

beta_one = 0.9
beta_two = 0.999
learn_rate = 0.05
adam_eps = 1e-08
score_eps = 1e-05

NX, NY, NZ, RUN = 4, 8, 16, 8
POP = 16
ROWS = 224
COLS = 512
KEEP = 2048
SLOT = 2 * ROWS + 16
T_Y, T_C, T_C4, T_X, T_SIB, T_P = 3.3, 3.0, 4.5, 3.0, 2.0, 13.0


def device_at(x, y, z, c):
    x, y, z = (x + NX) % NX, (y + NY) % NY, (z + NZ) % NZ
    return (y * 2 + z // RUN, (x * RUN + z % RUN) * 2 + c)


def swap_lanes(even, odd):
    low = lax.broadcasted_iota(jnp.int32, (even.shape[0], 128), 1) < 64
    parts = [[], []]
    for t in range(8):
        a = even[:, t * 128 : (t + 1) * 128]
        b = odd[:, t * 128 : (t + 1) * 128]
        parts[0].append(jnp.where(low, a, pltpu.roll(b, 64, 1)))
        parts[1].append(jnp.where(low, pltpu.roll(a, 64, 1), b))
    return jnp.concatenate(parts[0] + parts[1], axis=1)


def kernel(
    row_hbm, col_hbm, score_hbm, out_ref,
    row_ref, col_ref, score_ref, rowbuf, tags, colbuf, row_out, col_out, col_in, wbuf, acc, part_in,
    sem_in, sem_sib_s, sem_sib_r, sem_z8_s, sem_z8_r, sem_tag_s, sem_tag_r, sem_y_s, sem_y_r,
    sem_c_s, sem_c_r, sem_x_s, sem_x_r, sem_f_s, sem_f_r,
):
    p = lax.axis_index("pop")
    f = lax.axis_index("fsdp")
    y, zh = p // 2, p % 2
    c, zl, x = f % 2, (f // 2) % RUN, f // (2 * RUN)
    z = zh * RUN + zl
    turn = 1 - 2 * c
    upper, lower = zh == 1, zh == 0

    loads = [
        pltpu.make_async_copy(src, dst, sem_in.at[i])
        for i, (src, dst) in enumerate(((row_hbm, row_ref), (score_hbm, score_ref), (col_hbm, col_ref)))
    ]
    for load in loads:
        load.start()

    sibling = device_at(x, y, z, 1 - c)
    partner = device_at(x, y, z + 8, c)
    barrier = pltpu.get_barrier_semaphore()

    def greet(dev):
        pl.semaphore_signal(barrier, inc=1, device_id=dev, device_id_type=MESH)

    greet(sibling)
    for dev in (device_at(x, y + 1, z, c), device_at(x, y - 1, z, c), device_at(x + 1, y, z, c), device_at(x - 1, y, z, c)):
        greet(dev)
    pl.when(zl < 7)(lambda: greet(device_at(x, y, z + 1, c)))
    pl.when(zl < 4)(lambda: greet(device_at(x, y, z + 4, c)))
    pl.when(lower)(lambda: greet(partner))
    expected = 5 + jnp.where(zl > 0, 1, 0) + jnp.where(zl >= 4, 1, 0) + zh

    first_len = ROWS + 16
    own_rows = pl.multiple_of(c * first_len, 16)
    loads[0].wait()
    loads[1].wait()
    rows = jnp.swapaxes(row_ref[...], 0, 1)
    halves = [rows[2 * q : 2 * q + 2].reshape(128, ROWS).T for q in range(2)]
    rowbuf[p, pl.ds(own_rows, ROWS), :] = jnp.where(c == 0, halves[0], halves[1])
    row_out[...] = jnp.where(c == 0, halves[1], halves[0])
    score = score_ref[...]
    score = jnp.concatenate([score, score], axis=1)
    line = lax.broadcasted_iota(jnp.int32, (16, 128), 0)
    coded = jnp.where(line == 0, score // 16, jnp.where(line == 1, score % 16, 0))
    rowbuf[p, ROWS : ROWS + 16, :] = coded.astype(jnp.float32).astype(jnp.bfloat16)

    pl.semaphore_wait(barrier, expected)

    early, late = [], []

    def remote(src, dst, s_sem, r_sem, dev):
        return pltpu.make_async_remote_copy(
            src_ref=src, dst_ref=dst, send_sem=s_sem, recv_sem=r_sem, device_id=dev, device_id_type=MESH
        )

    def only(when, fn):
        if when is None:
            fn()
        else:
            pl.when(when)(fn)

    def go(copy, when=None, group=early):
        only(when, copy.start)
        group.append((when, copy))

    def piece(slot, stream, n):
        if n == 1:
            start, length = (1 - c) * first_len, ROWS
        elif stream == 0:
            start, length = c * ROWS, first_len
        else:
            start, length = c * first_len, ROWS
        return rowbuf.at[slot, pl.ds(pl.multiple_of(start, 16), length)]

    def y_copy(stream, way, hop, n):
        d = turn if way == 0 else -turn
        src_y = (y - d * (hop - 1) + 2 * NY) % NY
        ref = piece(src_y * 2 + (zh if stream == 0 else 1 - zh), stream, n)
        i = stream * 2 + way
        return remote(ref, ref, sem_y_s.at[i, hop - 1, n], sem_y_r.at[i, hop - 1, n], device_at(x, y + d, z, c))

    def z8_copy(n):
        ref = piece(p, 1, n)
        return remote(ref, ref, sem_z8_s.at[n], sem_z8_r.at[n], partner)

    own_tag = rowbuf.at[p, pl.ds(ROWS, 16)]
    tag_over = remote(own_tag, tags.at[y], sem_tag_s.at[0], sem_tag_r.at[0], partner)

    def tag_copy(k):
        return remote(tags.at[y], tags.at[y], sem_tag_s.at[k], sem_tag_r.at[k], device_at(x, y + k, z, c))

    def col_block(x_at, zl_at, half=None):
        at = pl.ds(pl.multiple_of((x_at * RUN + zl_at) * 16, 16), 16)
        if half is None:
            return colbuf.at[at]
        return colbuf.at[at, pl.ds(half * (KEEP // 2), KEEP // 2)]

    def inside(v):
        return jnp.logical_and(v >= 0, v < RUN)

    def c_send(way, d):
        step = 1 - 2 * way
        origin = zl - step * (0 if d == 4 else d - 1)
        jump = step * (4 if d == 4 else 1)
        ref = col_block(x, origin)
        copy = remote(
            ref, ref, sem_c_s.at[way, d - 1], sem_c_r.at[way, d - 1], device_at(x, y, z + jump, c)
        )
        go(copy, jnp.logical_and(inside(origin), inside(zl + jump)))

    def x_copy(way, x_at, zl_at, half=None):
        at = jnp.clip(zl_at, 0, RUN - 1)
        ref = col_block(x_at, zl_at, half)
        s, r = (sem_x_s, sem_x_r) if half is None else (sem_f_s, sem_f_r)
        return remote(ref, ref, s.at[way, at], r.at[way, at], device_at(x + 1 - 2 * way, y, z, c))

    def x_send(zl_at, when):
        for way in range(2):
            go(x_copy(way, x, zl_at), when)

    def x_pass(zl_at, when):
        for way in range(2):
            x_at = (x - (1 - 2 * way) + NX) % NX
            only(when, x_copy(way, x_at, zl_at).wait_recv)
            go(x_copy(way, x_at, zl_at, way), when)

    events = []

    def at_time(t, fn, *args):
        events.append((t, len(events), functools.partial(fn, *args)))

    sib_rows = remote(row_out, rowbuf.at[p, pl.ds(own_rows, ROWS)], sem_sib_s.at[0], sem_sib_r.at[0], sibling)
    sib_cols = remote(col_out, col_in, sem_sib_s.at[1], sem_sib_r.at[1], sibling)

    go(sib_rows)
    go(tag_over, upper)
    go(z8_copy(0), upper)
    go(y_copy(0, 0, 1, 0))
    go(y_copy(0, 1, 1, 0))
    loads[2].wait()
    blocks = [col_ref[k].astype(jnp.float32) for k in range(4)]
    wide = [swap_lanes(blocks[2 * q], blocks[2 * q + 1]) for q in range(2)]
    my_cols = jnp.where(c == 0, wide[0], wide[1])
    col_out[...] = jnp.where(c == 0, wide[1], wide[0]).astype(jnp.bfloat16)
    go(sib_cols)
    sib_rows.wait_recv()
    go(z8_copy(1), upper)
    go(y_copy(0, 0, 1, 1))
    go(y_copy(0, 1, 1, 1))

    def columns():
        sib_cols.wait_recv()
        other = col_in[...].astype(jnp.float32)
        both = jnp.concatenate([jnp.where(c == 0, my_cols, other), jnp.where(c == 0, other, my_cols)], axis=0)
        col_block(x, zl)[...] = both.astype(jnp.bfloat16)
        c_send(1, 1)
        c_send(1, 4)
        x_send(zl, None)

    at_time(T_SIB, columns)
    at_time(T_SIB + T_X, x_pass, zl, None)

    def y_event(stream, way, hop, n):
        y_copy(stream, way, hop, n).wait_recv()
        if hop < (4 if way == 0 else 3):
            go(y_copy(stream, way, hop + 1, n), group=late if stream else early)

    def tag_event():
        tag_over.wait_recv()
        for k in range(1, NY):
            go(tag_copy(k), group=late)
        go(tag_over, lower, late)
        go(z8_copy(0), lower, late)
        go(z8_copy(1), lower, late)

    def z8_event(n):
        z8_copy(n).wait_recv()
        go(y_copy(1, 0, 1, n), group=late)
        go(y_copy(1, 1, 1, n), group=late)

    at_time(T_P, tag_event)
    for n in range(2):
        at_time(T_P + 0.2 + n, z8_event, n)
        for stream in range(2):
            base = (0.0, T_P + 0.2)[stream] + n * (1.5, 1.0)[stream]
            for hop in range(1, 5):
                for way in range(2):
                    if hop <= (4 if way == 0 else 3):
                        at_time(base + T_Y * hop, y_event, stream, way, hop, n)

    def c_event(way, d):
        origin = zl - (1 - 2 * way) * d
        valid = inside(origin)
        ref = col_block(x, origin)
        only(valid, remote(ref, ref, sem_c_s.at[way, d - 1], sem_c_r.at[way, d - 1], sibling).wait_recv)
        if d not in (3, 7):
            c_send(way, d + 1)
        x_send(origin, valid)
        if way == 1 and d in (1, 4):
            c_send(0, d)

    def x_event(way, d):
        origin = zl - (1 - 2 * way) * d
        x_pass(origin, inside(origin))

    for d in range(1, 8):
        t = T_SIB + (T_C * d if d < 4 else T_C4 + T_C * (d - 4))
        for way, t_at in ((1, t), (0, t + (T_C if d < 4 else T_C4))):
            at_time(t_at, c_event, way, d)
            at_time(t_at + T_X, x_event, way, d)

    def halves_in():
        for way in range(2):
            for zl_at in range(RUN):
                x_copy(way, (x + 2) % NX, zl_at, way).wait_recv()

    def scores_of(tag):
        tag = tag.astype(jnp.float32)
        return tag[0:1] * 16.0 + tag[1:2]

    stats = []

    def totals():
        for k in range(1, NY):
            tag_copy(k).wait_recv()
        values = [scores_of(rowbuf[2 * i + zh, ROWS : ROWS + 16, :]) for i in range(NY)]
        values += [scores_of(tags[i]) for i in range(NY)]
        values = jnp.concatenate(values, axis=0)
        members = POP * 64
        average = jnp.sum(values) * 0.5 / members
        variance = jnp.sum(values * values) * 0.5 / members - average * average
        stats.extend((average, lax.rsqrt(variance + score_eps)))

    def weighted(slot, tag, h):
        fitness = (scores_of(tag) - stats[0]) * stats[1]
        block = rowbuf[slot, pl.ds(pl.multiple_of(h * first_len, 16), ROWS), :].astype(jnp.float32)
        return (block * fitness).astype(jnp.bfloat16)

    def times_columns(rows, first, width):
        return lax.dot_general(
            rows, colbuf[:, pl.ds(pl.multiple_of(first, 128), width)], (((1,), (1,)), ((), ())),
            preferred_element_type=jnp.float32,
        )

    def own_half():
        for i in range(NY):
            slot = 2 * i + zh
            tag = rowbuf[slot, ROWS : ROWS + 16, :]
            for h in range(2):
                wbuf[h, :, i * 128 : (i + 1) * 128] = weighted(slot, tag, h)
        for h in range(2):
            acc[h] = times_columns(wbuf[h], zh * (KEEP // 2), KEEP // 2)

    def add_block(y_at, h):
        slot = 2 * y_at + 1 - zh
        acc[h] += times_columns(weighted(slot, tags[y_at], h), (1 - zh) * (KEEP // 2) + y_at * 128, 128)

    def add_far(*hops):
        for hop in hops:
            for y_at in {0: (y,), 4: ((y - 4 * turn + NY) % NY,)}.get(
                hop, ((y - hop * turn + NY) % NY, (y + hop * turn + NY) % NY)
            ):
                for h in range(2):
                    add_block(y_at, h)

    t_last = T_P + 0.2 + 1.0
    t_cols = T_SIB + 2 * T_C4 + 3 * T_C + T_X
    at_time(t_cols, halves_in)
    at_time(t_cols, totals)
    at_time(t_cols, own_half)
    at_time(t_last + T_Y * 3 + 0.1, add_far, 0, 1, 2, 3)

    def departed(group):
        for when, copy in group:
            only(when, copy.wait_send)

    at_time(t_last + T_Y * 3 + 0.2, lambda: departed(early))

    for _, _, fn in sorted(events, key=lambda e: e[:2]):
        fn()

    last = (y - 4 * turn + NY) % NY
    add_block(last, 1 - c)
    swap = remote(acc.at[1 - c], part_in, sem_sib_s.at[2], sem_sib_r.at[2], sibling)
    swap.start()
    add_block(last, c)
    departed(late)
    swap.wait()
    out_ref[...] = (acc[c] + part_in[...]) * (1.0 / 64.0)


def local(weight, first_moment, second_moment, row_factors, column_factors, scores):
    columns = jnp.transpose(column_factors, (1, 2, 0))
    dma = pltpu.SemaphoreType.DMA
    update = pl.pallas_call(
        kernel,
        name="gather_update",
        out_shape=jax.ShapeDtypeStruct((ROWS, COLS), jnp.float32),
        in_specs=[pl.BlockSpec(memory_space=pltpu.HBM)] * 3,
        out_specs=pl.BlockSpec(memory_space=pltpu.VMEM),
        scratch_shapes=[
            pltpu.VMEM((64, 4, ROWS), jnp.bfloat16),
            pltpu.VMEM((4, 8, 1024), jnp.bfloat16),
            pltpu.VMEM((1, 64), jnp.int32),
            pltpu.VMEM((POP, SLOT, 128), jnp.bfloat16),
            pltpu.VMEM((NY, 16, 128), jnp.bfloat16),
            pltpu.VMEM((COLS, KEEP), jnp.bfloat16),
            pltpu.VMEM((ROWS, 128), jnp.bfloat16),
            pltpu.VMEM((8, KEEP), jnp.bfloat16),
            pltpu.VMEM((8, KEEP), jnp.bfloat16),
            pltpu.VMEM((2, ROWS, KEEP // 2), jnp.bfloat16),
            pltpu.VMEM((2, ROWS, COLS), jnp.float32),
            pltpu.VMEM((ROWS, COLS), jnp.float32),
            dma((3,)),
            dma((3,)), dma((3,)),
            dma((2,)), dma((2,)),
            dma((NY,)), dma((NY,)),
            dma((4, 4, 2)), dma((4, 4, 2)),
            dma((2, 7)), dma((2, 7)),
            dma((2, RUN)), dma((2, RUN)),
            dma((2, RUN)), dma((2, RUN)),
        ],
        compiler_params=pltpu.CompilerParams(
            collective_id=0, has_side_effects=True, vmem_limit_bytes=60 * 2**20
        ),
        cost_estimate=pl.CostEstimate(flops=2 * ROWS * COLS * 4096, bytes_accessed=2**20, transcendentals=0),
    )(row_factors, columns, scores.reshape(1, 64))
    new_first = beta_one * first_moment + (1.0 - beta_one) * update
    new_second = beta_two * second_moment + (1.0 - beta_two) * update * update
    corrected_first = new_first / (1.0 - beta_one**ADAM_STEP)
    corrected_second = new_second / (1.0 - beta_two**ADAM_STEP)
    new_weight = weight + learn_rate * corrected_first / (jnp.sqrt(corrected_second) + adam_eps)
    return (new_weight, new_first, new_second)


def solution(mesh):
    in_specs = (
        P("fsdp", "pop"),
        P("fsdp", "pop"),
        P("fsdp", "pop"),
        P("pop", None, "fsdp"),
        P(None, None, ("pop", "fsdp")),
        P("pop"),
    )
    out_specs = (P("fsdp", "pop"), P("fsdp", "pop"), P("fsdp", "pop"))
    return jax.shard_map(local, mesh=mesh, in_specs=in_specs, out_specs=out_specs, check_vma=False)
```

```python
import functools
import math

import jax
import jax.numpy as jnp
from jax import lax
from jax.experimental import pallas as pl
from jax.experimental.pallas import tpu as pltpu
from jax.sharding import PartitionSpec as P

ADAM_STEP = 10
MESH = pl.DeviceIdType.MESH

beta_one = 0.9
beta_two = 0.999
learn_rate = 0.05
adam_eps = 1e-08
score_eps = 1e-05

NX, NY, NZ, RUN = 4, 8, 16, 8
POP = 16
ROWS = 224
COLS = 512
DEPTH = 4096
TAG = 16
SLOT = TAG + 2 * ROWS
T_Y, T_C, T_HOP, T_X, T_COL, T_P = 2.9, 3.0, 0.5, 3.0, 2.0, 15.0
DIRECT, HALF, SPLIT = 5, 0.7, 0
PARENT = ({1: 0, 4: 0, 2: 1, 3: 2, 5: 4, 6: 5, 7: 6},) * 2


def device_at(x, y, z, c):
    x, y, z = (x + NX) % NX, (y + NY) % NY, (z + NZ) % NZ
    return (y * 2 + z // RUN, (x * RUN + z % RUN) * 2 + c)


def ordered(ranks):
    low = lax.broadcasted_iota(jnp.int32, (8, 128), 1) < 64
    parts = [[], []]
    for t in range(8):
        for q in range(2):
            a = ranks[2 * q][:, t * 128 : (t + 1) * 128]
            b = ranks[2 * q + 1][:, t * 128 : (t + 1) * 128]
            parts[0].append(jnp.where(low, a, pltpu.roll(b, 64, 1)))
            parts[1].append(jnp.where(low, pltpu.roll(a, 64, 1), b))
    return jnp.concatenate(parts[0] + parts[1], axis=1)


def kernel(
    row_hbm, col_hbm, score_hbm, out_ref,
    row_ref, col_ref, score_ref, rowbuf, tags, colbuf, col_out, col_in, wbuf, acc,
    sem_in, sem_sib_s, sem_sib_r, sem_z8_s, sem_z8_r, sem_tag_s, sem_tag_r, sem_y_s, sem_y_r,
    sem_push_s, sem_push_r, sem_pc_s, sem_pc_r, sem_c_s, sem_c_r, sem_x_s, sem_x_r, sem_f_s, sem_f_r, sem_ack,
):
    p = lax.axis_index("pop")
    f = lax.axis_index("fsdp")
    y, zh = p // 2, p % 2
    c, zl, x = f % 2, (f // 2) % RUN, f // (2 * RUN)
    z = zh * RUN + zl
    upper, lower = zh == 1, zh == 0
    column_core, row_core = c == 0, c == 1

    loads = [
        pltpu.make_async_copy(src, dst, sem_in.at[i])
        for i, (src, dst) in enumerate(((row_hbm, row_ref), (score_hbm, score_ref), (col_hbm, col_ref)))
    ]
    for load in loads:
        load.start()

    sibling = device_at(x, y, z, 1 - c)
    far_rows = device_at(x, y, z + 8, 1)
    barrier = pltpu.get_barrier_semaphore()

    def greet(*dev):
        pl.semaphore_signal(barrier, inc=1, device_id=device_at(*dev), device_id_type=MESH)

    greet(x, y, z, 1 - c)

    @pl.when(column_core)
    def _():
        greet(x + 1, y, z, 0)
        greet(x - 1, y, z, 0)
        pl.when(zl < 7)(lambda: greet(x, y, z + 1, 0))
        pl.when(zl < 4)(lambda: greet(x, y, z + 4, 0))
        if PARENT[1][2] == 0:
            pl.when(zl < 6)(lambda: greet(x, y, z + 2, 0))

    @pl.when(row_core)
    def _():
        greet(x, y + 1, z, 1)
        greet(x, y - 1, z, 1)

        @pl.when(lower)
        def _():
            greet(x, y, z + 8, 0)
            greet(x, y, z + 8, 1)

    below = jnp.where(zl > 0, 1, 0) + jnp.where(zl >= 4, 1, 0)
    if PARENT[1][2] == 0:
        below = below + jnp.where(zl >= 2, 1, 0)
    expected = 3 + zh + jnp.where(column_core, below, 0)

    loads[0].wait()
    loads[1].wait()
    rows = row_ref[...].astype(jnp.float32)
    own_rows = pl.multiple_of(TAG + c * ROWS, 16)
    for q in range(2):
        rowbuf[q, p, pl.ds(own_rows, ROWS), :] = jnp.concatenate([rows[:, 2 * q, :], rows[:, 2 * q + 1, :]], axis=0).T.astype(jnp.bfloat16)
    score = score_ref[...]
    score = jnp.concatenate([score, score], axis=1)
    line = lax.broadcasted_iota(jnp.int32, (TAG, 128), 0)
    coded = jnp.where(line == 0, score // 16, jnp.where(line == 1, score % 16, 0))
    rowbuf[0, p, 0:TAG, :] = coded.astype(jnp.float32).astype(jnp.bfloat16)

    pl.semaphore_wait(barrier, expected)

    def remote(src, dst, s_sem, r_sem, dev):
        return pltpu.make_async_remote_copy(
            src_ref=src, dst_ref=dst, send_sem=s_sem, recv_sem=r_sem, device_id=dev, device_id_type=MESH
        )

    def only(when, fn):
        if when is None:
            fn()
        else:
            pl.when(when)(fn)

    def inside(v):
        return jnp.logical_and(v >= 0, v < RUN)

    def z8_copy(q, n):
        ref = rowbuf.at[q, p, pl.ds(TAG + n * ROWS, ROWS)]
        return remote(ref, ref, sem_z8_s.at[q, n], sem_z8_r.at[q, n], far_rows)

    sib_rows = remote(
        rowbuf.at[:, p, pl.ds(TAG, ROWS)], rowbuf.at[:, p, pl.ds(TAG, ROWS)], sem_sib_s.at[0], sem_sib_r.at[0], sibling
    )
    sib_cols = remote(col_out, col_in, sem_sib_s.at[1], sem_sib_r.at[1], sibling)

    def own_columns():
        loads[2].wait()
        return ordered([col_ref[k].astype(jnp.float32) for k in range(4)])

    def scores_of(tag):
        tag = tag.astype(jnp.float32)
        return tag[0:1] * 16.0 + tag[1:2]

    def totals():
        values = [scores_of(rowbuf[0, 2 * i + zh, 0:TAG, :]) for i in range(NY)]
        values += [scores_of(tags[i]) for i in range(NY)]
        values = jnp.concatenate(values, axis=0)
        members = POP * 64
        average = jnp.sum(values) * 0.5 / members
        variance = jnp.sum(values * values) * 0.5 / members - average * average
        return average, lax.rsqrt(variance + score_eps)

    def weighted(slot, tag, stats):
        fitness = (scores_of(tag) - stats[0]) * stats[1]
        blocks = [rowbuf[q, slot, pl.ds(own_rows, ROWS), :].astype(jnp.float32) * fitness for q in range(2)]
        return jnp.concatenate(blocks, axis=1).astype(jnp.bfloat16)

    def times_columns(first, width):
        at = pl.ds(pl.multiple_of(first, 128), width)
        return lax.dot_general(
            wbuf[:, at], colbuf[:, at], (((1,), (1,)), ((), ())), preferred_element_type=jnp.float32
        )

    def weigh_own(stats):
        for i in range(NY):
            slot = 2 * i + zh
            wbuf[:, pl.ds(pl.multiple_of(zh * (DEPTH // 2) + i * 256, 256), 256)] = weighted(
                slot, rowbuf[0, slot, 0:TAG, :], stats
            )

    def weigh(y_at, stats):
        at = pl.ds(pl.multiple_of((1 - zh) * (DEPTH // 2) + y_at * 256, 256), 256)
        wbuf[:, at] = weighted(2 * y_at + 1 - zh, tags[y_at], stats)

    def hops_of(q, way):
        return 4 if q == way else 3

    def source_y(way, hop):
        return (y - (1 - 2 * way) * hop + NY) % NY

    def slot_of(stream, y_at):
        return y_at * 2 + (zh if stream == 0 else 1 - zh)

    def push(stream, q, y_at, sem):
        at = pl.ds(0, TAG + ROWS) if stream == 0 and q == 0 else pl.ds(TAG, ROWS)
        ref = rowbuf.at[q, slot_of(stream, y_at), at]
        return remote(ref, ref, sem_push_s.at[sem], sem_push_r.at[sem], sibling)

    tag_push = remote(tags, tags, sem_push_s.at[4], sem_push_r.at[4], sibling)

    class Schedule:
        def __init__(self):
            self.sent, self.events = [], []

        def go(self, copy, when=None):
            only(when, copy.start)
            self.sent.append((when, copy))

        def at(self, t, fn, *args):
            self.events.append((t, len(self.events), functools.partial(fn, *args)))

        def run(self):
            for _, _, fn in sorted(self.events, key=lambda e: e[:2]):
                fn()

        def departed(self):
            for when, copy in self.sent:
                only(when, copy.wait_send)
            self.sent = []

    def weigh_near(stats):
        for hop in range(4):
            for way in range(2 if hop else 1):
                weigh(source_y(way, hop), stats)

    @pl.when(row_core)
    def _():
        s = Schedule()
        own_tag = rowbuf.at[0, p, pl.ds(0, TAG)]
        tag_over = remote(own_tag, tags.at[y], sem_tag_s.at[0], sem_tag_r.at[0], far_rows)

        def tag_copy(k):
            return remote(tags.at[y], tags.at[y], sem_tag_s.at[k], sem_tag_r.at[k], device_at(x, y + k, z, 1))

        def y_copy(stream, q, way, hop, n=None):
            if n is None:
                at = pl.ds(0, SLOT) if stream == 0 and q == 0 else pl.ds(TAG, 2 * ROWS)
            else:
                at = pl.ds(TAG + n * ROWS, ROWS)
            ref = rowbuf.at[q, slot_of(stream, source_y(way, hop - 1)), at]
            i = stream * 2 + q + (2 if n == 1 else 0)
            return remote(
                ref, ref, sem_y_s.at[i, way, hop - 1], sem_y_r.at[i, way, hop - 1], device_at(x, y + 1 - 2 * way, z, 1)
            )

        s.go(tag_over, upper)
        s.go(z8_copy(0, 1), upper)
        s.go(z8_copy(1, 1), upper)
        col_out[...] = own_columns().astype(jnp.bfloat16)
        s.go(sib_cols)
        sib_rows.wait_recv()
        for q in range(2):
            for way in range(2):
                s.go(y_copy(0, q, way, 1))

        def y_event(stream, q, way, hop, n=None):
            y_copy(stream, q, way, hop, n).wait_recv()
            if hop < hops_of(q, way):
                s.go(y_copy(stream, q, way, hop + 1, n))
            if n == 1:
                return
            if stream == 0:
                sem = 0
            else:
                sem = 1 if hop < 4 else 2 + q
            s.go(push(stream, q, source_y(way, hop), sem))

        def tag_event():
            tag_over.wait_recv()
            for k in range(1, NY):
                s.go(tag_copy(k))
            s.go(tag_over, lower)
            for q in range(2):
                for n in range(2):
                    s.go(z8_copy(q, n), lower)

        def z8_event(q):
            if not SPLIT:
                for n in range(2):
                    z8_copy(q, n).wait_recv()
                for way in range(2):
                    s.go(y_copy(1, q, way, 1))
            else:
                for n in (1, 0):
                    z8_copy(q, n).wait_recv()
                    for way in range(2):
                        s.go(y_copy(1, q, way, 1, n))
            s.go(push(1, q, y, 1))

        def tags_in():
            for k in range(1, NY):
                tag_copy(k).wait_recv()
            s.go(tag_push)

        s.at(T_P, tag_event)
        s.at(T_P + 5.0, tags_in)
        for q in range(2):
            s.at(T_P + 0.5 + q * 0.5, z8_event, q)
            for stream in range(2):
                base = (2.0, T_P + 0.5)[stream] + 0.5 * q
                for hop in range(1, 5):
                    for way in range(2):
                        if hop <= hops_of(q, way):
                            for n in (1, 0) if stream and SPLIT else (None,):
                                s.at(base + T_Y * hop, y_event, stream, q, way, hop, n)
        s.run()
        stats = totals()
        weigh_own(stats)
        weigh_near(stats)
        weigh(source_y(0, 4), stats)
        remote(colbuf, colbuf, sem_pc_s, sem_pc_r, sibling).wait_recv()
        out_ref[...] = times_columns(0, DEPTH) * (1.0 / 64.0)
        s.departed()

    @pl.when(column_core)
    def _():
        s = Schedule()

        def col_block(x_at, zl_at, half=None):
            at = pl.ds(pl.multiple_of((x_at * RUN + zl_at) * 16, 16), 16)
            if half is None:
                return colbuf.at[at]
            return colbuf.at[at, pl.ds(half * (DEPTH // 2), DEPTH // 2)]

        def push_block(x_at, zl_at, when, half=None):
            ref = col_block(x_at, zl_at, half)
            s.go(remote(ref, ref, sem_pc_s, sem_pc_r, sibling), when)

        def c_send(way, d, half):
            step = 1 - 2 * way
            origin = zl - step * PARENT[way][d]
            jump = step * (d - PARENT[way][d])
            ref = col_block(x, origin, half)
            copy = remote(
                ref, ref, sem_c_s.at[way, d - 1, half], sem_c_r.at[way, d - 1, half], device_at(x, y, z + jump, 0)
            )
            s.go(copy, jnp.logical_and(inside(origin), inside(zl + jump)))

        def x_copy(way, x_at, zl_at, half):
            at = jnp.clip(zl_at, 0, RUN - 1)
            ref = col_block(x_at, zl_at, half)
            return remote(
                ref, ref, sem_x_s.at[way, at, half], sem_x_r.at[way, at, half], device_at(x + 1 - 2 * way, y, z, 0)
            )

        def far_copy(zl_at, half, x_at, straight):
            at = jnp.clip(zl_at, 0, RUN - 1)
            ref = col_block(x_at, zl_at, half)
            to = device_at(x + (2 if straight else 1 - 2 * half), y, z, 0)
            return remote(ref, ref, sem_f_s.at[at, half], sem_f_r.at[at, half], to)

        def x_send(zl_at, when, half, straight):
            for way in range(2):
                s.go(x_copy(way, x, zl_at, half), when)
            if straight:
                s.go(far_copy(zl_at, half, x, True), when)

        def x_pass(zl_at, when, half, straight):
            for way in (half, 1 - half):
                x_at = (x - (1 - 2 * way) + NX) % NX
                only(when, x_copy(way, x_at, zl_at, half).wait_recv)
                if way == half and not straight:
                    s.go(far_copy(zl_at, half, x_at, False), when)
                push_block(x_at, zl_at, when, half)

        pl.when(zl > 0)(
            lambda: pl.semaphore_signal(sem_ack.at[0], inc=1, device_id=device_at(x, y, z - 1, 0), device_id_type=MESH)
        )
        pl.when(zl >= 4)(
            lambda: pl.semaphore_signal(sem_ack.at[1], inc=1, device_id=device_at(x, y, z - 4, 0), device_id_type=MESH)
        )
        for q in range(2):
            s.go(z8_copy(q, 0), upper)
        s.go(sib_rows)
        mine = own_columns()
        sib_cols.wait_recv()
        both = jnp.concatenate([mine, col_in[...].astype(jnp.float32)], axis=0)
        col_block(x, zl)[...] = both.astype(jnp.bfloat16)
        for half in range(2):
            c_send(1, 1, half)
            x_send(zl, None, half, DIRECT <= 0)
        for d in (4, 2):
            if PARENT[1][d] == 0:
                c_send(1, d, 0)
                c_send(1, d, 1)
        for half in range(2):
            push_block(x, zl, None, half)

        def up_near():
            pl.when(zl < 7)(lambda: pl.semaphore_wait(sem_ack.at[0], 1))
            for half in range(2):
                c_send(0, 1, half)

        def up_far():
            pl.when(zl < 4)(lambda: pl.semaphore_wait(sem_ack.at[1], 1))
            for half in range(2):
                c_send(0, 4, half)

        def c_event(way, d, half):
            origin = zl - (1 - 2 * way) * d
            valid = inside(origin)
            ref = col_block(x, origin, half)
            only(valid, remote(ref, ref, sem_c_s.at[way, d - 1, half], sem_c_r.at[way, d - 1, half], sibling).wait_recv)
            for e in range(d + 1, RUN):
                if PARENT[way][e] == d:
                    c_send(way, e, half)
            x_send(origin, valid, half, d >= DIRECT)
            push_block(x, origin, valid, half)

        def x_event(way, d, half):
            origin = zl - (1 - 2 * way) * d
            x_pass(origin, inside(origin), half, d >= DIRECT)

        s.at(T_COL + 0.1, up_near)
        s.at(T_COL + 1.5, up_far)
        for half in range(2):
            s.at(T_COL + T_X + HALF * half, x_pass, zl, None, half, DIRECT <= 0)
            for way in range(2):
                arrives = {0: T_COL + HALF * half + 0.7 * (1 - way)}
                for d in range(1, RUN):
                    before = PARENT[way][d]
                    arrives[d] = arrives[before] + T_C + T_HOP * (d - before - 1)
                    s.at(arrives[d], c_event, way, d, half)
                    s.at(arrives[d] + T_X, x_event, way, d, half)
        s.run()
        for zl_at in range(RUN):
            for way in range(2):
                far_copy(zl_at, way, (x + 2) % NX, True).wait_recv()
                push_block((x + 2) % NX, zl_at, None, way)
        remote(
            rowbuf.at[0, pl.ds(0, 7)], rowbuf.at[0, pl.ds(0, 7)], sem_push_s.at[0], sem_push_r.at[0], sibling
        ).wait_recv()
        tag_push.wait_recv()
        stats = totals()
        weigh_own(stats)
        acc[...] = times_columns(zh * (DEPTH // 2), DEPTH // 2)
        most = rowbuf.at[:, pl.ds(0, 7), pl.ds(TAG, ROWS)]
        remote(most, most, sem_push_s.at[1], sem_push_r.at[1], sibling).wait_recv()
        weigh_near(stats)
        for q in range(2):
            push(1, q, source_y(q, 4), 2 + q).wait_recv()
        weigh(source_y(0, 4), stats)
        out_ref[...] = (acc[...] + times_columns((1 - zh) * (DEPTH // 2), DEPTH // 2)) * (1.0 / 64.0)
        s.departed()


def local(weight, first_moment, second_moment, row_factors, column_factors, scores):
    columns = jnp.transpose(column_factors, (1, 2, 0))
    dma = pltpu.SemaphoreType.DMA
    update = pl.pallas_call(
        kernel,
        name="gather_update",
        out_shape=jax.ShapeDtypeStruct((ROWS, COLS), jnp.float32),
        in_specs=[pl.BlockSpec(memory_space=pltpu.HBM)] * 3,
        out_specs=pl.BlockSpec(memory_space=pltpu.VMEM),
        scratch_shapes=[
            pltpu.VMEM((64, 4, ROWS), jnp.bfloat16),
            pltpu.VMEM((4, 8, 1024), jnp.bfloat16),
            pltpu.VMEM((1, 64), jnp.int32),
            pltpu.VMEM((2, POP, SLOT, 128), jnp.bfloat16),
            pltpu.VMEM((NY, TAG, 128), jnp.bfloat16),
            pltpu.VMEM((COLS, DEPTH), jnp.bfloat16),
            pltpu.VMEM((8, DEPTH), jnp.bfloat16),
            pltpu.VMEM((8, DEPTH), jnp.bfloat16),
            pltpu.VMEM((ROWS, DEPTH), jnp.bfloat16),
            pltpu.VMEM((ROWS, COLS), jnp.float32),
            dma((3,)),
            dma((2,)), dma((2,)),
            dma((2, 2)), dma((2, 2)),
            dma((NY,)), dma((NY,)),
            dma((6, 2, 4)), dma((6, 2, 4)),
            dma((5,)), dma((5,)),
            dma, dma,
            dma((2, 7, 2)), dma((2, 7, 2)),
            dma((2, RUN, 2)), dma((2, RUN, 2)),
            dma((RUN, 2)), dma((RUN, 2)),
            pltpu.SemaphoreType.REGULAR((2,)),
        ],
        compiler_params=pltpu.CompilerParams(
            collective_id=0, has_side_effects=True, vmem_limit_bytes=60 * 2**20
        ),
        cost_estimate=pl.CostEstimate(flops=2 * ROWS * COLS * 4096, bytes_accessed=2**20, transcendentals=0),
    )(row_factors, columns, scores.reshape(1, 64))
    new_first = beta_one * first_moment + (1.0 - beta_one) * update
    new_second = beta_two * second_moment + (1.0 - beta_two) * update * update
    corrected_first = new_first / (1.0 - beta_one**ADAM_STEP)
    corrected_second = new_second / (1.0 - beta_two**ADAM_STEP)
    new_weight = weight + learn_rate * corrected_first / (jnp.sqrt(corrected_second) + adam_eps)
    return (new_weight, new_first, new_second)


def solution(mesh):
    in_specs = (
        P("fsdp", "pop"),
        P("fsdp", "pop"),
        P("fsdp", "pop"),
        P("pop", None, "fsdp"),
        P(None, None, ("pop", "fsdp")),
        P("pop"),
    )
    out_specs = (P("fsdp", "pop"), P("fsdp", "pop"), P("fsdp", "pop"))
    return jax.shard_map(local, mesh=mesh, in_specs=in_specs, out_specs=out_specs, check_vma=False)
```

```python
import functools
import math

import jax
import jax.numpy as jnp
from jax import lax
from jax.experimental import pallas as pl
from jax.experimental.pallas import tpu as pltpu
from jax.sharding import PartitionSpec as P

ADAM_STEP = 10
MESH = pl.DeviceIdType.MESH

beta_one = 0.9
beta_two = 0.999
learn_rate = 0.05
adam_eps = 1e-08
score_eps = 1e-05

NX, NY, NZ, RUN = 4, 8, 16, 8
POP = 16
ROWS = 224
COLS = 512
DEPTH = 4096
TAG = 16
SLOT = TAG + 2 * ROWS
T_Y, T_C, T_HOP, T_X, T_COL, T_P = 2.9, 3.0, 0.5, 3.0, 2.0, 15.0
T_FAR = 4.0
DIRECT, HALF, SPLIT = 5, 0.7, 0
PARENT = ({1: 0, 4: 0, 2: 1, 3: 2, 5: 4, 6: 5, 7: 6},) * 2


def device_at(x, y, z, c):
    x, y, z = (x + NX) % NX, (y + NY) % NY, (z + NZ) % NZ
    return (y * 2 + z // RUN, (x * RUN + z % RUN) * 2 + c)


def ordered(ranks):
    low = lax.broadcasted_iota(jnp.int32, (8, 128), 1) < 64
    parts = [[], []]
    for t in range(8):
        for q in range(2):
            a = ranks[2 * q][:, t * 128 : (t + 1) * 128]
            b = ranks[2 * q + 1][:, t * 128 : (t + 1) * 128]
            parts[0].append(jnp.where(low, a, pltpu.roll(b, 64, 1)))
            parts[1].append(jnp.where(low, pltpu.roll(a, 64, 1), b))
    return jnp.concatenate(parts[0] + parts[1], axis=1)


def kernel(
    row_hbm, col_hbm, score_hbm, out_ref,
    row_ref, col_ref, score_ref, rowbuf, tags, colbuf, col_out, col_in, wbuf, acc,
    sem_in, sem_sib_s, sem_sib_r, sem_z8_s, sem_z8_r, sem_tag_s, sem_tag_r, sem_y_s, sem_y_r,
    sem_push_s, sem_push_r, sem_pc_s, sem_pc_r, sem_c_s, sem_c_r, sem_x_s, sem_x_r, sem_f_s, sem_f_r, sem_ack,
):
    p = lax.axis_index("pop")
    f = lax.axis_index("fsdp")
    y, zh = p // 2, p % 2
    c, zl, x = f % 2, (f // 2) % RUN, f // (2 * RUN)
    z = zh * RUN + zl
    upper, lower = zh == 1, zh == 0
    column_core, row_core = c == 0, c == 1

    loads = [
        pltpu.make_async_copy(src, dst, sem_in.at[i])
        for i, (src, dst) in enumerate(((row_hbm, row_ref), (score_hbm, score_ref), (col_hbm, col_ref)))
    ]
    for load in loads:
        load.start()

    sibling = device_at(x, y, z, 1 - c)
    far_rows = device_at(x, y, z + 8, 1)
    barrier = pltpu.get_barrier_semaphore()

    def greet(*dev):
        pl.semaphore_signal(barrier, inc=1, device_id=device_at(*dev), device_id_type=MESH)

    greet(x, y, z, 1 - c)

    @pl.when(column_core)
    def _():
        greet(x + 1, y, z, 0)
        greet(x - 1, y, z, 0)
        pl.when(zl < 7)(lambda: greet(x, y, z + 1, 0))
        pl.when(zl < 4)(lambda: greet(x, y, z + 4, 0))
        if PARENT[1][2] == 0:
            pl.when(zl < 6)(lambda: greet(x, y, z + 2, 0))

    @pl.when(row_core)
    def _():
        greet(x, y + 1, z, 1)
        greet(x, y - 1, z, 1)

        @pl.when(lower)
        def _():
            greet(x, y, z + 8, 0)
            greet(x, y, z + 8, 1)

    below = jnp.where(zl > 0, 1, 0) + jnp.where(zl >= 4, 1, 0)
    if PARENT[1][2] == 0:
        below = below + jnp.where(zl >= 2, 1, 0)
    expected = 3 + zh + jnp.where(column_core, below, 0)

    loads[0].wait()
    loads[1].wait()
    rows = row_ref[...].astype(jnp.float32)
    own_rows = pl.multiple_of(TAG + c * ROWS, 16)
    for q in range(2):
        rowbuf[q, p, pl.ds(own_rows, ROWS), :] = jnp.concatenate([rows[:, 2 * q, :], rows[:, 2 * q + 1, :]], axis=0).T.astype(jnp.bfloat16)
    score = score_ref[...]
    score = jnp.concatenate([score, score], axis=1)
    line = lax.broadcasted_iota(jnp.int32, (TAG, 128), 0)
    coded = jnp.where(line == 0, score // 16, jnp.where(line == 1, score % 16, 0))
    rowbuf[0, p, 0:TAG, :] = coded.astype(jnp.float32).astype(jnp.bfloat16)

    pl.semaphore_wait(barrier, expected)

    def remote(src, dst, s_sem, r_sem, dev):
        return pltpu.make_async_remote_copy(
            src_ref=src, dst_ref=dst, send_sem=s_sem, recv_sem=r_sem, device_id=dev, device_id_type=MESH
        )

    def only(when, fn):
        if when is None:
            fn()
        else:
            pl.when(when)(fn)

    def inside(v):
        return jnp.logical_and(v >= 0, v < RUN)

    def z8_copy(q, n):
        ref = rowbuf.at[q, p, pl.ds(TAG + n * ROWS, ROWS)]
        return remote(ref, ref, sem_z8_s.at[q, n], sem_z8_r.at[q, n], far_rows)

    sib_rows = remote(
        rowbuf.at[:, p, pl.ds(TAG, ROWS)], rowbuf.at[:, p, pl.ds(TAG, ROWS)], sem_sib_s.at[0], sem_sib_r.at[0], sibling
    )
    sib_cols = remote(col_out, col_in, sem_sib_s.at[1], sem_sib_r.at[1], sibling)

    def own_columns():
        loads[2].wait()
        return ordered([col_ref[k].astype(jnp.float32) for k in range(4)])

    def scores_of(tag):
        tag = tag.astype(jnp.float32)
        return tag[0:1] * 16.0 + tag[1:2]

    def totals():
        values = [scores_of(rowbuf[0, 2 * i + zh, 0:TAG, :]) for i in range(NY)]
        values += [scores_of(tags[i]) for i in range(NY)]
        values = jnp.concatenate(values, axis=0)
        members = POP * 64
        average = jnp.sum(values) * 0.5 / members
        variance = jnp.sum(values * values) * 0.5 / members - average * average
        return average, lax.rsqrt(variance + score_eps)

    def weighted(slot, tag, stats):
        fitness = (scores_of(tag) - stats[0]) * stats[1]
        blocks = [rowbuf[q, slot, pl.ds(own_rows, ROWS), :].astype(jnp.float32) * fitness for q in range(2)]
        return jnp.concatenate(blocks, axis=1).astype(jnp.bfloat16)

    def times_columns(first, width):
        at = pl.ds(pl.multiple_of(first, 128), width)
        return lax.dot_general(
            wbuf[:, at], colbuf[:, at], (((1,), (1,)), ((), ())), preferred_element_type=jnp.float32
        )

    def weigh_own(stats):
        for i in range(NY):
            slot = 2 * i + zh
            wbuf[:, pl.ds(pl.multiple_of(zh * (DEPTH // 2) + i * 256, 256), 256)] = weighted(
                slot, rowbuf[0, slot, 0:TAG, :], stats
            )

    def weigh(y_at, stats):
        at = pl.ds(pl.multiple_of((1 - zh) * (DEPTH // 2) + y_at * 256, 256), 256)
        wbuf[:, at] = weighted(2 * y_at + 1 - zh, tags[y_at], stats)

    def hops_of(q, way):
        return 4 if q == way else 3

    def source_y(way, hop):
        return (y - (1 - 2 * way) * hop + NY) % NY

    def slot_of(stream, y_at):
        return y_at * 2 + (zh if stream == 0 else 1 - zh)

    def push(stream, q, y_at, sem):
        at = pl.ds(0, TAG + ROWS) if stream == 0 and q == 0 else pl.ds(TAG, ROWS)
        ref = rowbuf.at[q, slot_of(stream, y_at), at]
        return remote(ref, ref, sem_push_s.at[sem], sem_push_r.at[sem], sibling)

    tag_push = remote(tags, tags, sem_push_s.at[4], sem_push_r.at[4], sibling)

    class Schedule:
        def __init__(self):
            self.sent, self.events = [], []

        def go(self, copy, when=None):
            only(when, copy.start)
            self.sent.append((when, copy))

        def at(self, t, fn, *args):
            self.events.append((t, len(self.events), functools.partial(fn, *args)))

        def run(self):
            for _, _, fn in sorted(self.events, key=lambda e: e[:2]):
                fn()

        def departed(self):
            for when, copy in self.sent:
                only(when, copy.wait_send)
            self.sent = []

    def weigh_near(stats):
        for hop in range(4):
            for way in range(2 if hop else 1):
                weigh(source_y(way, hop), stats)

    @pl.when(row_core)
    def _():
        s = Schedule()
        own_tag = rowbuf.at[0, p, pl.ds(0, TAG)]
        tag_over = remote(own_tag, tags.at[y], sem_tag_s.at[0], sem_tag_r.at[0], far_rows)

        def tag_copy(k):
            return remote(tags.at[y], tags.at[y], sem_tag_s.at[k], sem_tag_r.at[k], device_at(x, y + k, z, 1))

        def y_copy(stream, q, way, hop, n=None):
            if n is None:
                at = pl.ds(0, SLOT) if stream == 0 and q == 0 else pl.ds(TAG, 2 * ROWS)
            else:
                at = pl.ds(TAG + n * ROWS, ROWS)
            ref = rowbuf.at[q, slot_of(stream, source_y(way, hop - 1)), at]
            i = stream * 2 + q + (2 if n == 1 else 0)
            return remote(
                ref, ref, sem_y_s.at[i, way, hop - 1], sem_y_r.at[i, way, hop - 1], device_at(x, y + 1 - 2 * way, z, 1)
            )

        s.go(tag_over, upper)
        s.go(z8_copy(0, 1), upper)
        s.go(z8_copy(1, 1), upper)
        col_out[...] = own_columns().astype(jnp.bfloat16)
        s.go(sib_cols)
        sib_rows.wait_recv()
        for q in range(2):
            for way in range(2):
                s.go(y_copy(0, q, way, 1))

        def y_event(stream, q, way, hop, n=None):
            y_copy(stream, q, way, hop, n).wait_recv()
            if hop < hops_of(q, way):
                s.go(y_copy(stream, q, way, hop + 1, n))
            if n == 1:
                return
            if stream == 0:
                sem = 0
            else:
                sem = 1 if hop < 4 else 2 + q
            s.go(push(stream, q, source_y(way, hop), sem))

        def tag_event():
            tag_over.wait_recv()
            for k in range(1, NY):
                s.go(tag_copy(k))
            s.go(tag_over, lower)
            for q in range(2):
                for n in range(2):
                    s.go(z8_copy(q, n), lower)

        def z8_event(q):
            if not SPLIT:
                for n in range(2):
                    z8_copy(q, n).wait_recv()
                for way in range(2):
                    s.go(y_copy(1, q, way, 1))
            else:
                for n in (1, 0):
                    z8_copy(q, n).wait_recv()
                    for way in range(2):
                        s.go(y_copy(1, q, way, 1, n))
            s.go(push(1, q, y, 1))

        def tags_in():
            for k in range(1, NY):
                tag_copy(k).wait_recv()
            s.go(tag_push)

        s.at(T_P, tag_event)
        s.at(T_P + 5.0, tags_in)
        for q in range(2):
            s.at(T_P + 0.5 + q * 0.5, z8_event, q)
            for stream in range(2):
                base = (2.0, T_P + 0.5)[stream] + 0.5 * q
                for hop in range(1, 5):
                    for way in range(2):
                        if hop <= hops_of(q, way):
                            for n in (1, 0) if stream and SPLIT else (None,):
                                s.at(base + T_Y * hop, y_event, stream, q, way, hop, n)
        s.run()
        stats = totals()
        weigh_own(stats)
        weigh_near(stats)
        weigh(source_y(0, 4), stats)
        remote(colbuf, colbuf, sem_pc_s, sem_pc_r, sibling).wait_recv()
        out_ref[...] = times_columns(0, DEPTH) * (1.0 / 64.0)
        s.departed()

    @pl.when(column_core)
    def _():
        s = Schedule()

        def col_block(x_at, zl_at, half=None):
            at = pl.ds(pl.multiple_of((x_at * RUN + zl_at) * 16, 16), 16)
            if half is None:
                return colbuf.at[at]
            return colbuf.at[at, pl.ds(half * (DEPTH // 2), DEPTH // 2)]

        def push_block(x_at, zl_at, when, half=None):
            ref = col_block(x_at, zl_at, half)
            s.go(remote(ref, ref, sem_pc_s, sem_pc_r, sibling), when)

        def c_send(way, d, half):
            step = 1 - 2 * way
            origin = zl - step * PARENT[way][d]
            jump = step * (d - PARENT[way][d])
            ref = col_block(x, origin, half)
            copy = remote(
                ref, ref, sem_c_s.at[way, d - 1, half], sem_c_r.at[way, d - 1, half], device_at(x, y, z + jump, 0)
            )
            s.go(copy, jnp.logical_and(inside(origin), inside(zl + jump)))

        def x_copy(way, x_at, zl_at, half):
            at = jnp.clip(zl_at, 0, RUN - 1)
            ref = col_block(x_at, zl_at, half)
            return remote(
                ref, ref, sem_x_s.at[way, at, half], sem_x_r.at[way, at, half], device_at(x + 1 - 2 * way, y, z, 0)
            )

        def far_copy(zl_at, half, x_at, straight):
            at = jnp.clip(zl_at, 0, RUN - 1)
            ref = col_block(x_at, zl_at, half)
            to = device_at(x + (2 if straight else 1 - 2 * half), y, z, 0)
            return remote(ref, ref, sem_f_s.at[at, half], sem_f_r.at[at, half], to)

        def x_send(zl_at, when, half, straight):
            for way in range(2):
                s.go(x_copy(way, x, zl_at, half), when)
            if straight:
                s.go(far_copy(zl_at, half, x, True), when)

        def x_pass(zl_at, when, half, straight):
            for way in (half, 1 - half):
                x_at = (x - (1 - 2 * way) + NX) % NX
                only(when, x_copy(way, x_at, zl_at, half).wait_recv)
                if way == half and not straight:
                    s.go(far_copy(zl_at, half, x_at, False), when)
                push_block(x_at, zl_at, when, half)

        pl.when(zl > 0)(
            lambda: pl.semaphore_signal(sem_ack.at[0], inc=1, device_id=device_at(x, y, z - 1, 0), device_id_type=MESH)
        )
        pl.when(zl >= 4)(
            lambda: pl.semaphore_signal(sem_ack.at[1], inc=1, device_id=device_at(x, y, z - 4, 0), device_id_type=MESH)
        )
        for q in range(2):
            s.go(z8_copy(q, 0), upper)
        s.go(sib_rows)
        mine = own_columns()
        sib_cols.wait_recv()
        both = jnp.concatenate([mine, col_in[...].astype(jnp.float32)], axis=0)
        col_block(x, zl)[...] = both.astype(jnp.bfloat16)
        for half in range(2):
            c_send(1, 1, half)
            x_send(zl, None, half, DIRECT <= 0)
        for d in (4, 2):
            if PARENT[1][d] == 0:
                c_send(1, d, 0)
                c_send(1, d, 1)
        for half in range(2):
            push_block(x, zl, None, half)

        def up_near():
            pl.when(zl < 7)(lambda: pl.semaphore_wait(sem_ack.at[0], 1))
            for half in range(2):
                c_send(0, 1, half)

        def up_far():
            pl.when(zl < 4)(lambda: pl.semaphore_wait(sem_ack.at[1], 1))
            for half in range(2):
                c_send(0, 4, half)

        def c_event(way, d, half):
            origin = zl - (1 - 2 * way) * d
            valid = inside(origin)
            ref = col_block(x, origin, half)
            only(valid, remote(ref, ref, sem_c_s.at[way, d - 1, half], sem_c_r.at[way, d - 1, half], sibling).wait_recv)
            for e in range(d + 1, RUN):
                if PARENT[way][e] == d:
                    c_send(way, e, half)
            x_send(origin, valid, half, d >= DIRECT)
            push_block(x, origin, valid, half)

        def x_event(way, d, half):
            origin = zl - (1 - 2 * way) * d
            x_pass(origin, inside(origin), half, d >= DIRECT)

        def far_in(zl_at, when, half):
            only(when, far_copy(zl_at, half, (x + 2) % NX, True).wait_recv)
            push_block((x + 2) % NX, zl_at, when, half)

        def far_event(way, d, half):
            origin = zl - (1 - 2 * way) * d
            far_in(origin, inside(origin), half)

        s.at(T_COL + 0.1, up_near)
        s.at(T_COL + 1.5, up_far)
        for half in range(2):
            s.at(T_COL + T_X + HALF * half, x_pass, zl, None, half, DIRECT <= 0)
            s.at(T_COL + T_X + HALF * half + T_FAR, far_in, zl, None, half)
            for way in range(2):
                arrives = {0: T_COL + HALF * half + 0.7 * (1 - way)}
                for d in range(1, RUN):
                    before = PARENT[way][d]
                    arrives[d] = arrives[before] + T_C + T_HOP * (d - before - 1)
                    s.at(arrives[d], c_event, way, d, half)
                    s.at(arrives[d] + T_X, x_event, way, d, half)
                    s.at(arrives[d] + T_X + T_FAR, far_event, way, d, half)
        s.run()
        remote(
            rowbuf.at[0, pl.ds(0, 7)], rowbuf.at[0, pl.ds(0, 7)], sem_push_s.at[0], sem_push_r.at[0], sibling
        ).wait_recv()
        tag_push.wait_recv()
        stats = totals()
        weigh_own(stats)
        acc[...] = times_columns(zh * (DEPTH // 2), DEPTH // 2)
        most = rowbuf.at[:, pl.ds(0, 7), pl.ds(TAG, ROWS)]
        remote(most, most, sem_push_s.at[1], sem_push_r.at[1], sibling).wait_recv()
        weigh_near(stats)
        for q in range(2):
            push(1, q, source_y(q, 4), 2 + q).wait_recv()
        weigh(source_y(0, 4), stats)
        out_ref[...] = (acc[...] + times_columns((1 - zh) * (DEPTH // 2), DEPTH // 2)) * (1.0 / 64.0)
        s.departed()


def local(weight, first_moment, second_moment, row_factors, column_factors, scores):
    columns = jnp.transpose(column_factors, (1, 2, 0))
    dma = pltpu.SemaphoreType.DMA
    update = pl.pallas_call(
        kernel,
        name="gather_update",
        out_shape=jax.ShapeDtypeStruct((ROWS, COLS), jnp.float32),
        in_specs=[pl.BlockSpec(memory_space=pltpu.HBM)] * 3,
        out_specs=pl.BlockSpec(memory_space=pltpu.VMEM),
        scratch_shapes=[
            pltpu.VMEM((64, 4, ROWS), jnp.bfloat16),
            pltpu.VMEM((4, 8, 1024), jnp.bfloat16),
            pltpu.VMEM((1, 64), jnp.int32),
            pltpu.VMEM((2, POP, SLOT, 128), jnp.bfloat16),
            pltpu.VMEM((NY, TAG, 128), jnp.bfloat16),
            pltpu.VMEM((COLS, DEPTH), jnp.bfloat16),
            pltpu.VMEM((8, DEPTH), jnp.bfloat16),
            pltpu.VMEM((8, DEPTH), jnp.bfloat16),
            pltpu.VMEM((ROWS, DEPTH), jnp.bfloat16),
            pltpu.VMEM((ROWS, COLS), jnp.float32),
            dma((3,)),
            dma((2,)), dma((2,)),
            dma((2, 2)), dma((2, 2)),
            dma((NY,)), dma((NY,)),
            dma((6, 2, 4)), dma((6, 2, 4)),
            dma((5,)), dma((5,)),
            dma, dma,
            dma((2, 7, 2)), dma((2, 7, 2)),
            dma((2, RUN, 2)), dma((2, RUN, 2)),
            dma((RUN, 2)), dma((RUN, 2)),
            pltpu.SemaphoreType.REGULAR((2,)),
        ],
        compiler_params=pltpu.CompilerParams(
            collective_id=0, has_side_effects=True, vmem_limit_bytes=60 * 2**20
        ),
        cost_estimate=pl.CostEstimate(flops=2 * ROWS * COLS * 4096, bytes_accessed=2**20, transcendentals=0),
    )(row_factors, columns, scores.reshape(1, 64))
    new_first = beta_one * first_moment + (1.0 - beta_one) * update
    new_second = beta_two * second_moment + (1.0 - beta_two) * update * update
    corrected_first = new_first / (1.0 - beta_one**ADAM_STEP)
    corrected_second = new_second / (1.0 - beta_two**ADAM_STEP)
    new_weight = weight + learn_rate * corrected_first / (jnp.sqrt(corrected_second) + adam_eps)
    return (new_weight, new_first, new_second)


def solution(mesh):
    in_specs = (
        P("fsdp", "pop"),
        P("fsdp", "pop"),
        P("fsdp", "pop"),
        P("pop", None, "fsdp"),
        P(None, None, ("pop", "fsdp")),
        P("pop"),
    )
    out_specs = (P("fsdp", "pop"), P("fsdp", "pop"), P("fsdp", "pop"))
    return jax.shard_map(local, mesh=mesh, in_specs=in_specs, out_specs=out_specs, check_vma=False)
```
